32 devices in a mesh: fsdp: 16 (over z, x, core), tp: 2 (over y).
Axes of the slice: x: 2, y: 2, z: 4, core: 2. Of those that a mesh axis runs over, the one named last changes fastest.
Arguments:
- hidden_in: bfloat16 [32, 512, 1024], P('fsdp', 'tp'), may hold values from -6 to 6
- segment_ids: int32 [32, 512], P('fsdp'), may hold values from 0 to 3, never falling along the last dimension, each value on 1 to 256 neighbouring positions
- norm_gain: bfloat16 [2, 1024], P(None, 'fsdp'), may hold values from 0.5 to 1.5
- norm_bias: bfloat16 [2, 1024], P(None, 'fsdp'), may hold values from -1.75 to 1.75
- qkv_weight: bfloat16 [1024, 3, 1024], P('fsdp', None, 'tp'), may hold values from -0.1875 to 0.1875
- qkv_bias: bfloat16 [3, 1024], P(None, ('tp', 'fsdp')), may hold values from -1.75 to 1.75
- dense_weight: bfloat16 [1024, 1024], P('fsdp', 'tp'), may hold values from -0.75 to 0.75
- mlp_in_weight: bfloat16 [1024, 4096], P('fsdp', 'tp'), may hold values from -0.1875 to 0.1875
- mlp_in_bias: bfloat16 [4096], P(('tp', 'fsdp')), may hold values from -1.75 to 1.75
- mlp_out_weight: bfloat16 [1024, 4096], P('fsdp', 'tp'), may hold values from -0.1875 to 0.1875
- out_bias: bfloat16 [2, 1024], P(None, 'fsdp'), may hold values from -1.75 to 1.75
- out_grad: bfloat16 [32, 512, 1024], P('fsdp', 'tp'), may hold values from -6 to 6
Outputs:
- hidden_out: bfloat16 [32, 512, 1024], P('fsdp', 'tp')
- input_grad: float32 [32, 512, 1024], P('fsdp', 'tp')
- norm_gain_grad: float32 [2, 1024], P(None, 'fsdp')
- norm_bias_grad: float32 [2, 1024], P(None, 'fsdp')
- qkv_weight_grad: float32 [1024, 3, 1024], P('fsdp', None, 'tp')
- qkv_bias_grad: float32 [3, 1024], P(None, ('tp', 'fsdp'))
- dense_weight_grad: float32 [1024, 1024], P('fsdp', 'tp')
- mlp_in_weight_grad: float32 [1024, 4096], P('fsdp', 'tp')
- mlp_in_bias_grad: float32 [4096], P(('tp', 'fsdp'))
- mlp_out_weight_grad: float32 [1024, 4096], P('fsdp', 'tp')
- out_bias_grad: float32 [2, 1024], P(None, 'fsdp')
The draws below stay inside these ranges and needn't reach their ends.
Inputs may be any that keep to these rules, and one draw needn't show every extreme that they name: `segment_ids`: within each row of 512 tokens the ids never fall, every id of 0 to 3 occurs as one run, and the longest run has exactly 256 tokens.
All inputs are finite; a program needn't handle non-finite values.
Results may differ from the reference program's by a relative error of at most 0.03.
Values may be sent and summed in bfloat16 or wider, within the bound.
A program may use at most 128 MiB of HBM per device.

```python
import math
import jax
import jax.numpy as jnp
import numpy as np
from jax import lax

D = 1024
HEADS = 16
HEAD_DIM = 64
FF = 4096
ROT_DIM = 16
ROW = 512
DOCS = 4
MOST_DOC = 256
NROWS = 32


def block_levels(key, shape, cuts, smallest, top_value):
    def one(axis_at, shards_of):
        draws = jax.random.uniform(jax.random.fold_in(jax.random.fold_in(key, 6), axis_at), (shards_of,), jnp.float32, smallest / len(cuts), top_value / len(cuts))
        return jnp.repeat(jnp.exp(draws), shape[axis_at] // shards_of).reshape((-1,) + (1,) * (len(shape) - axis_at - 1))

    loudness = one(*cuts[0])
    for cut in cuts[1:]:
        loudness = loudness * one(*cut)
    return loudness


def profile(amount, total, most, lean):
    weights = [(1 << 20) // math.isqrt(grade ** lean) + 1 for grade in range(2, amount + 1)]
    spare, holding = total - most - (amount - 1), [1] * (amount - 1)
    while spare > 0:
        free = [i for i in range(amount - 1) if holding[i] < most]
        whole, remaining = sum([weights[i] for i in free]), spare
        for i in free:
            more = min(most - holding[i], max(1, remaining * weights[i] // whole), spare)
            holding[i] = holding[i] + more
            spare = spare - more
    return np.array([most] + holding)


def uneven_parts(own_key, number_of, total, limit, skew):
    if number_of == 2:
        one = jax.random.randint(own_key, (), max(1, total - limit), min(limit, total - 1) + 1)
        return jnp.stack([one, total - one])
    sizes = jnp.asarray(profile(number_of, total, limit, skew), jnp.int32)
    couples = (number_of - 1) // 2
    source_of, taker = sizes[1:1 + 2 * couples:2], sizes[2:2 + 2 * couples:2]
    room = jnp.minimum(source_of - 1, limit - taker)
    moved = jax.random.randint(jax.random.fold_in(own_key, 1), (couples,), 0, 1 << 20) % (room + 1)
    sizes = sizes.at[1:1 + 2 * couples:2].set(source_of - moved).at[2:2 + 2 * couples:2].set(taker + moved)
    return sizes[jax.random.permutation(jax.random.fold_in(own_key, 2), number_of)]


def noise(stream_key, dims, deviation, reach, cuts=(), kind=jnp.bfloat16):
    result = jax.random.normal(stream_key, dims, jnp.float32) * deviation
    if len(cuts) > 0:
        result = block_levels(stream_key, dims, cuts, -0.22, 0.18) * result
    return jnp.clip(result, min=-reach, max=reach).astype(kind)


def setup_inputs(seed: int = 0) -> dict:
    streams_of = jax.random.split(jax.random.key(seed), 13)
    hidden_in = noise(streams_of[0], (NROWS, ROW, D), 1.0, 6.0, ((0, 16), (1, 2)))
    segment_ids = jax.vmap(lambda own: jnp.searchsorted(jnp.cumsum(uneven_parts(own, DOCS, ROW, MOST_DOC, 1)), jnp.arange(ROW), side="right"))(jax.random.split(streams_of[1], NROWS)).reshape((NROWS, ROW)).astype(jnp.int32)
    norm_gain = jnp.clip(1.0 + 0.1 * jax.random.normal(streams_of[2], (2, D), jnp.float32), 0.5, 1.5).astype(jnp.bfloat16)
    norm_bias = noise(streams_of[3], (2, D), 0.3, 1.75, ((1, 16),))
    qkv_weight = noise(streams_of[4], (D, 3, D), D ** -0.5, 0.1875, ((0, 16), (2, 2)))
    qkv_bias = noise(streams_of[5], (3, D), 0.3, 1.75, ((1, 32),))
    dense_weight = noise(streams_of[6], (D, D), (D // 16) ** -0.5, 0.75, ((0, 16), (1, 2)))
    mlp_in_weight = noise(streams_of[7], (D, FF), D ** -0.5, 0.1875, ((0, 16), (1, 2)))
    mlp_in_bias = noise(streams_of[8], (FF,), 0.3, 1.75, ((0, 32),))
    mlp_out_weight = noise(streams_of[9], (D, FF), (FF // 4) ** -0.5, 0.1875, ((0, 16), (1, 2)))
    out_bias = noise(streams_of[10], (2, D), 0.3, 1.75, ((1, 16),))
    out_grad = noise(streams_of[11], (NROWS, ROW, D), 1.0, 6.0, ((0, 16), (1, 2)))
    return dict(hidden_in=hidden_in, segment_ids=segment_ids, norm_gain=norm_gain, norm_bias=norm_bias, qkv_weight=qkv_weight, qkv_bias=qkv_bias, dense_weight=dense_weight, mlp_in_weight=mlp_in_weight, mlp_in_bias=mlp_in_bias, mlp_out_weight=mlp_out_weight, out_bias=out_bias, out_grad=out_grad)


@jax.custom_vjp
def low(v):
    return lax.optimization_barrier(v.astype(jnp.bfloat16)).astype(jnp.float32)

@jax.custom_vjp
def low_back(v):
    return v

def low_keep(v):
    return (low(v), None)

def low_pass(kept, grad):
    return (grad,)

def back_keep(v):
    return (v, None)

def back_low(kept, grad):
    return (low(grad),)
low.defvjp(low_keep, low_pass)
low_back.defvjp(back_keep, back_low)
norm_eps = 1e-05
highest = lax.Precision.HIGHEST
masked_fill = -1e+30

def layer_norm(row_values, gain_row, shift_row):
    average = lax.optimization_barrier(jnp.mean(row_values, axis=-1, keepdims=True))
    centered = row_values - average
    variance = lax.optimization_barrier(jnp.mean(centered * centered, axis=-1, keepdims=True))
    return centered * lax.rsqrt(variance + norm_eps) * gain_row + shift_row

def rotary_tables(segment_rows):
    row_width = segment_rows.shape[-1]
    places = jnp.arange(row_width, dtype=jnp.int32)
    same_doc = segment_rows[..., :, None] == segment_rows[..., None, :]
    allowed = jnp.logical_and(same_doc, places[None, :] <= places[:, None])
    positions = lax.optimization_barrier(jnp.sum(allowed.astype(jnp.int32), axis=-1)) - 1
    half_dim = ROT_DIM // 2
    frequency = jnp.exp(jnp.arange(half_dim, dtype=jnp.float32) * (-2.0 * math.log(10000.0) / ROT_DIM))
    angles = positions.astype(jnp.float32)[..., None] * frequency
    cosine_table = jnp.concatenate([jnp.cos(angles), jnp.cos(angles)], axis=-1)[..., None, :]
    sine_table = jnp.concatenate([jnp.sin(angles), jnp.sin(angles)], axis=-1)[..., None, :]
    return (cosine_table, sine_table, allowed)

def rotate(vectors, cosine_table, sine_table):
    half_dim = ROT_DIM // 2
    first_half = vectors[..., :half_dim]
    second_half = vectors[..., half_dim:ROT_DIM]
    flipped = jnp.concatenate([-second_half, first_half], axis=-1)
    turned = vectors[..., :ROT_DIM] * cosine_table + flipped * sine_table
    return jnp.concatenate([turned, vectors[..., ROT_DIM:]], axis=-1)

def layer_forward(hidden, norm_gain, norm_bias, qkv_weight, qkv_bias, dense_weight, mlp_in_weight, mlp_in_bias, mlp_out_weight, out_bias, cosine_table, sine_table, allowed):
    attn_in = low(layer_norm(hidden, norm_gain[0], norm_bias[0]))
    mlp_input = low(layer_norm(hidden, norm_gain[1], norm_bias[1]))
    projected = low_back(jnp.einsum('brd,dje->brje', attn_in, qkv_weight, precision=highest) + qkv_bias)
    head_shape = hidden.shape[:2] + (HEADS, HEAD_DIM)
    queries = low(rotate(projected[:, :, 0].reshape(head_shape), cosine_table, sine_table))
    key_rows = low(rotate(projected[:, :, 1].reshape(head_shape), cosine_table, sine_table))
    value_rows = low(projected[:, :, 2].reshape(head_shape))
    scores = low_back(jnp.einsum('bqhe,bkhe->bhqk', queries, key_rows, precision=highest) * HEAD_DIM ** (-0.5))
    weights = jax.nn.softmax(jnp.where(allowed[:, None], scores, masked_fill), axis=-1)
    mixed_rows = low_back(low(jnp.einsum('bhqk,bkhe->bqhe', low(weights), value_rows, precision=highest)))
    attn_out = jnp.einsum('brd,ed->bre', mixed_rows.reshape(hidden.shape), dense_weight, precision=highest)
    pre_act = low_back(jnp.einsum('brd,df->brf', mlp_input, mlp_in_weight, precision=highest) + mlp_in_bias)
    activated = low(jax.nn.gelu(pre_act, approximate=False))
    mlp_out = jnp.einsum('brf,ef->bre', activated, mlp_out_weight, precision=highest)
    branches = low_back(attn_out + mlp_out)
    return hidden + branches + out_bias[0] + out_bias[1]

def reference(hidden_in, segment_ids, norm_gain, norm_bias, qkv_weight, qkv_bias, dense_weight, mlp_in_weight, mlp_in_bias, mlp_out_weight, out_bias, out_grad):
    weights_all = tuple((array_in.astype(jnp.float32) for array_in in (norm_gain, norm_bias, qkv_weight, qkv_bias, dense_weight, mlp_in_weight, mlp_in_bias, mlp_out_weight, out_bias)))
    rows_total = hidden_in.shape[0]
    block_rows = math.gcd(rows_total, 8)
    blocks = rows_total // block_rows

    def into_blocks(array_in):
        return array_in.reshape((blocks, block_rows) + array_in.shape[1:])

    def one_block(totals, pieces):
        hidden_blk, segment_blk, grad_blk = pieces
        cosine_table, sine_table, allowed = rotary_tables(segment_blk)

        def forward(hidden_rows, *params):
            return layer_forward(hidden_rows, *params, cosine_table, sine_table, allowed)
        outputs, pull_back = jax.vjp(forward, hidden_blk.astype(jnp.float32), *weights_all)
        gradients = pull_back(grad_blk.astype(jnp.float32))
        totals = tuple((running_sum + new_grad for running_sum, new_grad in zip(totals, gradients[1:])))
        return (totals, (outputs.astype(jnp.bfloat16), gradients[0]))
    zero_sums = tuple((jnp.zeros_like(array_in) for array_in in weights_all))
    totals, (outputs, input_grads) = lax.scan(one_block, zero_sums, (into_blocks(hidden_in), into_blocks(segment_ids), into_blocks(out_grad)))
    return (outputs.reshape(hidden_in.shape), input_grads.reshape(hidden_in.shape), totals[0], totals[1], totals[2], totals[3], totals[4], totals[5], totals[6], totals[7], totals[8])
```

```python
import functools
import math

import jax
import jax.numpy as jnp
from jax import lax
from jax.experimental import pallas as pl
from jax.experimental.pallas import tpu as pltpu
from jax.sharding import PartitionSpec as P

HEAD_DIM = 64
ROT_DIM = 16
PAIR = 2 * HEAD_DIM


norm_eps = 1e-05
masked_fill = -1e30


def rotary_rows(segment_rows):
    row_width = segment_rows.shape[-1]
    places = jnp.arange(row_width, dtype=jnp.int32)
    same_doc = segment_rows[..., :, None] == segment_rows[..., None, :]
    allowed = jnp.logical_and(same_doc, places[None, :] <= places[:, None])
    positions = jnp.sum(allowed.astype(jnp.int32), axis=-1) - 1
    half_dim = ROT_DIM // 2
    frequency = jnp.exp(
        jnp.arange(half_dim, dtype=jnp.float32) * (-2.0 * math.log(10000.0) / ROT_DIM)
    )
    angles = positions.astype(jnp.float32)[..., None] * frequency
    cosine, sine = jnp.cos(angles), jnp.sin(angles)
    rest = HEAD_DIM - ROT_DIM
    ones = jnp.ones(angles.shape[:-1] + (rest,), jnp.float32)
    blank = jnp.zeros_like(ones)
    half_blank = jnp.zeros_like(sine)
    keep = jnp.concatenate([cosine, cosine, ones], axis=-1)
    ahead = jnp.concatenate([-sine, half_blank, blank], axis=-1)
    behind = jnp.concatenate([half_blank, sine, blank], axis=-1)
    return tuple(jnp.concatenate([part, part], axis=-1) for part in (keep, ahead, behind))


def attention_kernel(
    seg_row, seg_col, keep, ahead, behind, proj, mixed_grad, mixed_out, grad_out
):
    half_dim = ROT_DIM // 2
    scale = HEAD_DIM ** (-0.5)
    c, a, b = keep[0], ahead[0], behind[0]

    def turn(u):
        return u * c + pltpu.roll(u, PAIR - half_dim, 1) * a + pltpu.roll(u, half_dim, 1) * b

    def turn_back(w):
        return w * c - pltpu.roll(w, PAIR - half_dim, 1) * a - pltpu.roll(w, half_dim, 1) * b

    def dot(x, y, dims):
        return lax.dot_general(x, y, (dims, ((), ())), preferred_element_type=jnp.float32)

    queries = turn(proj[0]).astype(jnp.bfloat16)
    key_rows = turn(proj[1]).astype(jnp.bfloat16)
    value_rows = proj[2].astype(jnp.bfloat16)
    d_mixed = mixed_grad[...]
    row_len = queries.shape[0]
    lane = lax.broadcasted_iota(jnp.int32, (row_len, PAIR), 1)
    first = lane < HEAD_DIM
    q_place = lax.broadcasted_iota(jnp.int32, (row_len, row_len), 0)
    k_place = lax.broadcasted_iota(jnp.int32, (row_len, row_len), 1)
    allowed = jnp.logical_and(seg_row[0] == seg_col[0], k_place <= q_place)
    results = []
    for head in range(2):
        mine = first if head == 0 else jnp.logical_not(first)
        q_head = jnp.where(mine, queries, jnp.zeros_like(queries))
        d_head = jnp.where(mine, d_mixed, jnp.zeros_like(d_mixed))
        scores = dot(q_head, key_rows, ((1,), (1,))) * scale
        masked = jnp.where(allowed, scores, masked_fill)
        largest = jnp.max(masked, axis=-1, keepdims=True)
        expanded = jnp.exp(masked - largest)
        summed = jnp.sum(expanded, axis=-1, keepdims=True)
        weights = expanded * (1.0 / summed)
        low = weights.astype(jnp.bfloat16)
        mixed = dot(low, value_rows, ((1,), (0,)))
        weight_grad = dot(d_head, value_rows, ((1,), (1,)))
        inner = jnp.sum(weights * weight_grad, axis=-1, keepdims=True)
        score_grad = (weights * (weight_grad - inner)).astype(jnp.bfloat16)
        value_grad = dot(low, d_mixed, ((0,), (0,)))
        query_grad = dot(score_grad, key_rows, ((1,), (0,))) * scale
        key_grad = dot(score_grad, queries, ((0,), (0,))) * scale
        results.append((mixed, query_grad, key_grad, value_grad))
    mixed, query_grad, key_grad, value_grad = [
        jnp.where(first, one, two) for one, two in zip(*results)
    ]
    mixed_out[...] = mixed.astype(mixed_out.dtype)
    grad_out[0] = turn_back(query_grad).astype(grad_out.dtype)
    grad_out[1] = turn_back(key_grad).astype(grad_out.dtype)
    grad_out[2] = value_grad.astype(grad_out.dtype)


def attention(segment_ids, tables, proj, mixed_grad):
    seq_count, row_len = segment_ids.shape
    _, token_count, width = proj.shape
    pairs = width // PAIR
    table_spec = pl.BlockSpec((1, row_len, PAIR), lambda s, h: (s, 0, 0))
    flat_spec = pl.BlockSpec((row_len, PAIR), lambda s, h: (s, h))
    three_spec = pl.BlockSpec((3, row_len, PAIR), lambda s, h: (0, s, h))
    cells = seq_count * pairs * 2 * row_len * row_len
    return pl.pallas_call(
        attention_kernel,
        grid=(seq_count, pairs),
        in_specs=[
            pl.BlockSpec((1, 1, row_len), lambda s, h: (s, 0, 0)),
            pl.BlockSpec((1, row_len, 1), lambda s, h: (s, 0, 0)),
            table_spec,
            table_spec,
            table_spec,
            three_spec,
            flat_spec,
        ],
        out_specs=[flat_spec, three_spec],
        out_shape=[
            jax.ShapeDtypeStruct((token_count, width), jnp.bfloat16),
            jax.ShapeDtypeStruct((3, token_count, width), jnp.bfloat16),
        ],
        compiler_params=pltpu.CompilerParams(vmem_limit_bytes=40 * 2**20),
        cost_estimate=pl.CostEstimate(
            flops=cells * 12 * PAIR, bytes_accessed=proj.size * 8, transcendentals=cells
        ),
    )(segment_ids[:, None, :], segment_ids[:, :, None], *tables, proj, mixed_grad)


def join_rows(local, parts):
    if parts != 2:
        return lax.all_gather(local, "tp", axis=1, tiled=True)
    other = lax.ppermute(local, "tp", [(0, 1), (1, 0)])
    upper = lax.axis_index("tp") == 0
    return jnp.concatenate(
        [jnp.where(upper, local, other), jnp.where(upper, other, local)], axis=1
    )


def share_rows(partial, parts):
    if parts != 2:
        return lax.psum_scatter(
            partial.astype(jnp.bfloat16), "tp", scatter_dimension=1, tiled=True
        ).astype(jnp.float32)
    half = partial.shape[1] // 2
    mine = lax.axis_index("tp")
    away = lax.dynamic_slice_in_dim(partial, (1 - mine) * half, half, 1).astype(jnp.bfloat16)
    arrived = lax.ppermute(away, "tp", [(0, 1), (1, 0)])
    return lax.dynamic_slice_in_dim(partial, mine * half, half, 1) + arrived.astype(jnp.float32)


def pad_rows(values, width):
    groups, count = values.shape
    rows = -(-count // width)
    rows = -(-rows // 16) * 16
    return jnp.pad(values, ((0, 0), (0, rows * width - count))).reshape(groups, rows, width)


def on_device(
    shards,
    parts,
    hidden_in,
    segment_ids,
    norm_gain,
    norm_bias,
    qkv_weight,
    qkv_bias,
    dense_weight,
    mlp_in_weight,
    mlp_in_bias,
    mlp_out_weight,
    out_bias,
    out_grad,
):
    f32, bf16 = jnp.float32, jnp.bfloat16
    seq_count, local_len, model_width = hidden_in.shape
    row_len = segment_ids.shape[1]
    token_count = seq_count * row_len
    own_rows, _, local_width = qkv_weight.shape
    hidden = mlp_in_weight.shape[1]
    own_features = norm_gain.shape[1]
    own_bias, own_hidden = qkv_bias.shape[1], mlp_in_bias.shape[0]

    small = jnp.concatenate(
        [norm_gain.ravel(), norm_bias.ravel(), out_bias.ravel(), qkv_bias.ravel(), mlp_in_bias]
    )
    small_rows = pad_rows(small[None], hidden)[0]
    mlp_pack = lax.all_gather(
        jnp.concatenate([mlp_in_weight, mlp_out_weight, small_rows], axis=0), "fsdp", axis=0
    )
    rows = join_rows(hidden_in, parts).reshape(token_count, model_width).astype(f32)
    grad_flat = join_rows(out_grad, parts).reshape(token_count, model_width)
    attn_local = jnp.concatenate(
        [qkv_weight[:, 0], qkv_weight[:, 1], qkv_weight[:, 2], dense_weight], axis=0
    )
    mlp_pack, attn_local = lax.optimization_barrier((mlp_pack, attn_local))
    attn_pack = lax.all_gather(attn_local, "fsdp", axis=0)

    in_full = mlp_pack[:, :own_rows].reshape(model_width, hidden)
    out_full = mlp_pack[:, own_rows : 2 * own_rows].reshape(model_width, hidden)
    small_all = mlp_pack[:, 2 * own_rows :].reshape(shards, -1).astype(f32)
    features = small_all[:, : 6 * own_features].reshape(shards, 6, own_features)
    features = features.transpose(1, 0, 2).reshape(6, model_width)
    gains, shifts, out_shift = features[0:2], features[2:4], features[4:6]
    at = 6 * own_features
    qkv_shift = small_all[:, at : at + 3 * own_bias].reshape(shards, 3, own_bias)
    qkv_shift = qkv_shift.transpose(1, 0, 2).reshape(3, local_width)
    at = at + 3 * own_bias
    in_shift = small_all[:, at : at + own_hidden].reshape(hidden)

    centered = rows - jnp.mean(rows, axis=-1, keepdims=True)
    spread = lax.rsqrt(jnp.mean(centered * centered, axis=-1, keepdims=True) + norm_eps)
    xhat = centered * spread
    attn_flat = (xhat * gains[0] + shifts[0]).astype(bf16)
    mlp_flat = (xhat * gains[1] + shifts[1]).astype(bf16)

    pre_act = jnp.dot(mlp_flat, in_full, preferred_element_type=f32) + in_shift
    share = 0.5 * (1.0 + lax.erf(pre_act * math.sqrt(0.5)))
    act_low = (pre_act * share).astype(bf16)
    slope = (
        share + pre_act * jnp.exp(-0.5 * pre_act * pre_act) * (1.0 / math.sqrt(2.0 * math.pi))
    ).astype(bf16)
    act_grad = jnp.dot(grad_flat, out_full, preferred_element_type=f32)
    pre_grad = (act_grad * slope.astype(f32)).astype(bf16)
    in_weight_grad = jnp.einsum("nd,nf->df", mlp_flat, pre_grad, preferred_element_type=f32)
    out_weight_grad = jnp.einsum("nd,nf->df", grad_flat, act_low, preferred_element_type=f32)
    mlp_grads = jnp.concatenate(
        [
            in_weight_grad.astype(bf16).reshape(shards, own_rows, hidden),
            out_weight_grad.astype(bf16).reshape(shards, own_rows, hidden),
        ],
        axis=1,
    )
    mlp_grads, attn_pack = lax.optimization_barrier((mlp_grads, attn_pack))
    mlp_owned = lax.psum_scatter(mlp_grads, "fsdp", scatter_dimension=0, tiled=False)

    attn_parts = attn_pack.reshape(shards, 4, own_rows, local_width).transpose(1, 0, 2, 3)
    attn_parts = attn_parts.reshape(4, model_width, local_width)
    qkv_full, dense_full = attn_parts[0:3], attn_parts[3]
    proj = (
        jnp.einsum("nd,jde->jne", attn_flat, qkv_full, preferred_element_type=f32)
        + qkv_shift[:, None, :]
    )
    mixed_grad = jnp.dot(grad_flat, dense_full, preferred_element_type=f32).astype(bf16)
    mixed_flat, proj_grad = attention(segment_ids, rotary_rows(segment_ids), proj, mixed_grad)

    qkv_grad = jnp.einsum("nd,jne->jde", attn_flat, proj_grad, preferred_element_type=f32)
    dense_grad = jnp.einsum("nd,ne->de", grad_flat, mixed_flat, preferred_element_type=f32)
    attn_input_grad = jnp.einsum("jne,jde->nd", proj_grad, qkv_full, preferred_element_type=f32)
    mlp_input_grad = jnp.einsum("nf,df->nd", pre_grad, in_full, preferred_element_type=f32)
    normed_grad = (attn_input_grad * gains[0] + mlp_input_grad * gains[1]).reshape(
        seq_count, row_len, model_width
    )
    normed_grad = share_rows(normed_grad, parts)
    vectors = jnp.stack(
        [
            jnp.sum(attn_input_grad * xhat, axis=0),
            jnp.sum(mlp_input_grad * xhat, axis=0),
            jnp.sum(attn_input_grad, axis=0),
            jnp.sum(mlp_input_grad, axis=0),
            jnp.sum(out_grad.astype(f32), axis=(0, 1)),
        ]
    )
    if parts == 2:
        vectors = vectors + lax.ppermute(vectors, "tp", [(0, 1), (1, 0)])
    else:
        vectors = lax.psum(vectors, "tp")
    qkv_bias_grad = jnp.sum(proj_grad.astype(f32), axis=1)
    in_bias_grad = jnp.sum(pre_grad.astype(f32), axis=0)
    small_grads = jnp.concatenate(
        [
            vectors.reshape(5, shards, own_features).transpose(1, 0, 2).reshape(shards, -1),
            qkv_bias_grad.reshape(3, shards, own_bias).transpose(1, 0, 2).reshape(shards, -1),
            in_bias_grad.reshape(shards, own_hidden),
        ],
        axis=1,
    ).astype(bf16)
    attn_grads = jnp.concatenate(
        [qkv_grad[j].astype(bf16).reshape(shards, own_rows, local_width) for j in range(3)]
        + [dense_grad.astype(bf16).reshape(shards, own_rows, local_width)]
        + [pad_rows(small_grads, local_width)],
        axis=1,
    )
    attn_owned = lax.psum_scatter(attn_grads, "fsdp", scatter_dimension=0, tiled=False)

    attn_part = jnp.einsum("ne,de->nd", mixed_flat, dense_full, preferred_element_type=f32)
    mlp_part = jnp.einsum("nf,df->nd", act_low, out_full, preferred_element_type=f32)
    branches = share_rows((attn_part + mlp_part).reshape(seq_count, row_len, model_width), parts)
    local_rows = hidden_in.astype(f32)
    hidden_out = (local_rows + branches + out_shift[0] + out_shift[1]).astype(bf16)

    local_centered = local_rows - jnp.mean(local_rows, axis=-1, keepdims=True)
    local_spread = lax.rsqrt(
        jnp.mean(local_centered * local_centered, axis=-1, keepdims=True) + norm_eps
    )
    local_hat = local_centered * local_spread
    inner = jnp.mean(normed_grad * local_hat, axis=-1, keepdims=True)
    level = jnp.mean(normed_grad, axis=-1, keepdims=True)
    input_grad = out_grad.astype(f32) + (normed_grad - level - local_hat * inner) * local_spread

    owned = attn_owned[: 4 * own_rows].astype(f32).reshape(4, own_rows, local_width)
    small_owned = attn_owned[4 * own_rows :].astype(f32).ravel()
    vector_owned = small_owned[: 5 * own_features].reshape(5, own_features)
    at = 5 * own_features
    bias_owned = small_owned[at : at + 3 * own_bias].reshape(3, own_bias)
    at = at + 3 * own_bias
    hidden_owned = small_owned[at : at + own_hidden]
    return (
        hidden_out,
        input_grad,
        vector_owned[0:2],
        vector_owned[2:4],
        owned[0:3].transpose(1, 0, 2),
        bias_owned,
        owned[3],
        mlp_owned[:own_rows].astype(f32),
        hidden_owned,
        mlp_owned[own_rows:].astype(f32),
        jnp.stack([vector_owned[4], vector_owned[4]]),
    )


def solution(mesh):
    in_specs = (
        P("fsdp", "tp", None),
        P("fsdp", None),
        P(None, "fsdp"),
        P(None, "fsdp"),
        P("fsdp", None, "tp"),
        P(None, ("tp", "fsdp")),
        P("fsdp", "tp"),
        P("fsdp", "tp"),
        P(("tp", "fsdp")),
        P("fsdp", "tp"),
        P(None, "fsdp"),
        P("fsdp", "tp", None),
    )
    out_specs = (
        P("fsdp", "tp", None),
        P("fsdp", "tp", None),
        P(None, "fsdp"),
        P(None, "fsdp"),
        P("fsdp", None, "tp"),
        P(None, ("tp", "fsdp")),
        P("fsdp", "tp"),
        P("fsdp", "tp"),
        P(("tp", "fsdp")),
        P("fsdp", "tp"),
        P(None, "fsdp"),
    )
    return jax.shard_map(
        functools.partial(on_device, mesh.shape["fsdp"], mesh.shape["tp"]),
        mesh=mesh,
        in_specs=in_specs,
        out_specs=out_specs,
        check_vma=False,
    )
```

```python
import functools
import math

import jax
import jax.numpy as jnp
from jax import lax
from jax.experimental import pallas as pl
from jax.experimental.pallas import tpu as pltpu
from jax.sharding import PartitionSpec as P

HEAD_DIM = 64
ROT_DIM = 16
PAIR = 2 * HEAD_DIM


norm_eps = 1e-05
masked_fill = -1e30


def rotary_rows(segment_rows):
    row_width = segment_rows.shape[-1]
    places = jnp.arange(row_width, dtype=jnp.int32)
    same_doc = segment_rows[..., :, None] == segment_rows[..., None, :]
    allowed = jnp.logical_and(same_doc, places[None, :] <= places[:, None])
    positions = jnp.sum(allowed.astype(jnp.int32), axis=-1) - 1
    half_dim = ROT_DIM // 2
    frequency = jnp.exp(
        jnp.arange(half_dim, dtype=jnp.float32) * (-2.0 * math.log(10000.0) / ROT_DIM)
    )
    angles = positions.astype(jnp.float32)[..., None] * frequency
    cosine, sine = jnp.cos(angles), jnp.sin(angles)
    rest = HEAD_DIM - ROT_DIM
    ones = jnp.ones(angles.shape[:-1] + (rest,), jnp.float32)
    blank = jnp.zeros_like(ones)
    half_blank = jnp.zeros_like(sine)
    keep = jnp.concatenate([cosine, cosine, ones], axis=-1)
    ahead = jnp.concatenate([-sine, half_blank, blank], axis=-1)
    behind = jnp.concatenate([half_blank, sine, blank], axis=-1)
    return tuple(jnp.concatenate([part, part], axis=-1) for part in (keep, ahead, behind))


def attention_kernel(
    seg_row, seg_col, keep, ahead, behind, proj, mixed_grad, mixed_out, grad_out
):
    half_dim = ROT_DIM // 2
    scale = HEAD_DIM ** (-0.5)
    c, a, b = keep[0], ahead[0], behind[0]

    def turn(u):
        return u * c + pltpu.roll(u, PAIR - half_dim, 1) * a + pltpu.roll(u, half_dim, 1) * b

    def turn_back(w):
        return w * c - pltpu.roll(w, PAIR - half_dim, 1) * a - pltpu.roll(w, half_dim, 1) * b

    def dot(x, y, dims):
        return lax.dot_general(x, y, (dims, ((), ())), preferred_element_type=jnp.float32)

    queries = turn(proj[0]).astype(jnp.bfloat16)
    key_rows = turn(proj[1]).astype(jnp.bfloat16)
    value_rows = proj[2].astype(jnp.bfloat16)
    d_mixed = mixed_grad[...]
    row_len = queries.shape[0]
    lane = lax.broadcasted_iota(jnp.int32, (row_len, PAIR), 1)
    first = lane < HEAD_DIM
    q_place = lax.broadcasted_iota(jnp.int32, (row_len, row_len), 0)
    k_place = lax.broadcasted_iota(jnp.int32, (row_len, row_len), 1)
    allowed = jnp.logical_and(seg_row[0] == seg_col[0], k_place <= q_place)
    results = []
    for head in range(2):
        mine = first if head == 0 else jnp.logical_not(first)
        q_head = jnp.where(mine, queries, jnp.zeros_like(queries))
        d_head = jnp.where(mine, d_mixed, jnp.zeros_like(d_mixed))
        scores = dot(q_head, key_rows, ((1,), (1,))) * scale
        masked = jnp.where(allowed, scores, masked_fill)
        largest = jnp.max(masked, axis=-1, keepdims=True)
        expanded = jnp.exp(masked - largest)
        summed = jnp.sum(expanded, axis=-1, keepdims=True)
        weights = expanded * (1.0 / summed)
        low = weights.astype(jnp.bfloat16)
        mixed = dot(low, value_rows, ((1,), (0,)))
        weight_grad = dot(d_head, value_rows, ((1,), (1,)))
        inner = jnp.sum(weights * weight_grad, axis=-1, keepdims=True)
        score_grad = (weights * (weight_grad - inner)).astype(jnp.bfloat16)
        value_grad = dot(low, d_mixed, ((0,), (0,)))
        query_grad = dot(score_grad, key_rows, ((1,), (0,))) * scale
        key_grad = dot(score_grad, queries, ((0,), (0,))) * scale
        results.append((mixed, query_grad, key_grad, value_grad))
    mixed, query_grad, key_grad, value_grad = [
        jnp.where(first, one, two) for one, two in zip(*results)
    ]
    mixed_out[...] = mixed.astype(mixed_out.dtype)
    grad_out[0] = turn_back(query_grad).astype(grad_out.dtype)
    grad_out[1] = turn_back(key_grad).astype(grad_out.dtype)
    grad_out[2] = value_grad.astype(grad_out.dtype)


def attention(segment_ids, tables, proj, mixed_grad):
    seq_count, row_len = segment_ids.shape
    _, token_count, width = proj.shape
    pairs = width // PAIR
    table_spec = pl.BlockSpec((1, row_len, PAIR), lambda s, h: (s, 0, 0))
    flat_spec = pl.BlockSpec((row_len, PAIR), lambda s, h: (s, h))
    three_spec = pl.BlockSpec((3, row_len, PAIR), lambda s, h: (0, s, h))
    cells = seq_count * pairs * 2 * row_len * row_len
    return pl.pallas_call(
        attention_kernel,
        grid=(seq_count, pairs),
        in_specs=[
            pl.BlockSpec((1, 1, row_len), lambda s, h: (s, 0, 0)),
            pl.BlockSpec((1, row_len, 1), lambda s, h: (s, 0, 0)),
            table_spec,
            table_spec,
            table_spec,
            three_spec,
            flat_spec,
        ],
        out_specs=[flat_spec, three_spec],
        out_shape=[
            jax.ShapeDtypeStruct((token_count, width), jnp.bfloat16),
            jax.ShapeDtypeStruct((3, token_count, width), jnp.bfloat16),
        ],
        compiler_params=pltpu.CompilerParams(vmem_limit_bytes=40 * 2**20),
        cost_estimate=pl.CostEstimate(
            flops=cells * 12 * PAIR, bytes_accessed=proj.size * 8, transcendentals=cells
        ),
    )(segment_ids[:, None, :], segment_ids[:, :, None], *tables, proj, mixed_grad)


def join_rows(local, parts):
    if parts != 2:
        return lax.all_gather(local, "tp", axis=1, tiled=True)
    other = lax.ppermute(local, "tp", [(0, 1), (1, 0)])
    upper = lax.axis_index("tp") == 0
    return jnp.concatenate(
        [jnp.where(upper, local, other), jnp.where(upper, other, local)], axis=1
    )


def share_rows(partial, parts):
    if parts != 2:
        return lax.psum_scatter(
            partial.astype(jnp.bfloat16), "tp", scatter_dimension=1, tiled=True
        ).astype(jnp.float32)
    half = partial.shape[1] // 2
    mine = lax.axis_index("tp")
    away = lax.dynamic_slice_in_dim(partial, (1 - mine) * half, half, 1).astype(jnp.bfloat16)
    arrived = lax.ppermute(away, "tp", [(0, 1), (1, 0)])
    return lax.dynamic_slice_in_dim(partial, mine * half, half, 1) + arrived.astype(jnp.float32)


def pad_rows(values, width):
    groups, count = values.shape
    rows = -(-count // width)
    rows = -(-rows // 16) * 16
    return jnp.pad(values, ((0, 0), (0, rows * width - count))).reshape(groups, rows, width)


def on_device(
    shards,
    parts,
    hidden_in,
    segment_ids,
    norm_gain,
    norm_bias,
    qkv_weight,
    qkv_bias,
    dense_weight,
    mlp_in_weight,
    mlp_in_bias,
    mlp_out_weight,
    out_bias,
    out_grad,
):
    f32, bf16 = jnp.float32, jnp.bfloat16
    seq_count, local_len, model_width = hidden_in.shape
    row_len = segment_ids.shape[1]
    token_count = seq_count * row_len
    own_rows, _, local_width = qkv_weight.shape
    hidden = mlp_in_weight.shape[1]
    own_features = norm_gain.shape[1]
    own_bias, own_hidden = qkv_bias.shape[1], mlp_in_bias.shape[0]

    small = jnp.concatenate(
        [norm_gain.ravel(), norm_bias.ravel(), out_bias.ravel(), qkv_bias.ravel(), mlp_in_bias]
    )
    small_rows = pad_rows(small[None], hidden)[0]
    mlp_pack = lax.all_gather(
        jnp.concatenate([mlp_in_weight, mlp_out_weight, small_rows], axis=0), "fsdp", axis=0
    )
    rows = join_rows(hidden_in, parts).reshape(token_count, model_width).astype(f32)
    grad_flat = join_rows(out_grad, parts).reshape(token_count, model_width)
    attn_local = jnp.concatenate(
        [qkv_weight[:, 0], qkv_weight[:, 1], qkv_weight[:, 2], dense_weight], axis=0
    )
    mlp_pack, attn_local = lax.optimization_barrier((mlp_pack, attn_local))
    attn_pack = lax.all_gather(attn_local, "fsdp", axis=0)

    in_full = mlp_pack[:, :own_rows].reshape(model_width, hidden)
    out_full = mlp_pack[:, own_rows : 2 * own_rows].reshape(model_width, hidden)
    small_all = mlp_pack[:, 2 * own_rows :].reshape(shards, -1).astype(f32)
    features = small_all[:, : 6 * own_features].reshape(shards, 6, own_features)
    features = features.transpose(1, 0, 2).reshape(6, model_width)
    gains, shifts, out_shift = features[0:2], features[2:4], features[4:6]
    at = 6 * own_features
    qkv_shift = small_all[:, at : at + 3 * own_bias].reshape(shards, 3, own_bias)
    qkv_shift = qkv_shift.transpose(1, 0, 2).reshape(3, local_width)
    at = at + 3 * own_bias
    in_shift = small_all[:, at : at + own_hidden].reshape(hidden)

    centered = rows - jnp.mean(rows, axis=-1, keepdims=True)
    spread = lax.rsqrt(jnp.mean(centered * centered, axis=-1, keepdims=True) + norm_eps)
    xhat = centered * spread
    attn_flat = (xhat * gains[0] + shifts[0]).astype(bf16)
    mlp_flat = (xhat * gains[1] + shifts[1]).astype(bf16)

    pre_act = jnp.dot(mlp_flat, in_full, preferred_element_type=f32) + in_shift
    share = 0.5 * (1.0 + lax.erf(pre_act * math.sqrt(0.5)))
    act_low = (pre_act * share).astype(bf16)
    slope = (
        share + pre_act * jnp.exp(-0.5 * pre_act * pre_act) * (1.0 / math.sqrt(2.0 * math.pi))
    ).astype(bf16)
    act_grad = jnp.dot(grad_flat, out_full, preferred_element_type=f32)
    pre_grad = (act_grad * slope.astype(f32)).astype(bf16)
    in_weight_grad = jnp.einsum("nd,nf->df", mlp_flat, pre_grad, preferred_element_type=f32)
    out_weight_grad = jnp.einsum("nd,nf->df", grad_flat, act_low, preferred_element_type=f32)
    mlp_grads = jnp.concatenate(
        [
            in_weight_grad.astype(bf16).reshape(shards, own_rows, hidden),
            out_weight_grad.astype(bf16).reshape(shards, own_rows, hidden),
        ],
        axis=1,
    )
    mlp_grads, attn_pack = lax.optimization_barrier((mlp_grads, attn_pack))
    mlp_owned = lax.psum_scatter(
        mlp_grads.reshape(-1, hidden), "fsdp", scatter_dimension=0, tiled=True
    )

    attn_parts = attn_pack.reshape(shards, 4, own_rows, local_width).transpose(1, 0, 2, 3)
    attn_parts = attn_parts.reshape(4, model_width, local_width)
    qkv_full, dense_full = attn_parts[0:3], attn_parts[3]
    proj = (
        jnp.einsum("nd,jde->jne", attn_flat, qkv_full, preferred_element_type=f32)
        + qkv_shift[:, None, :]
    )
    mixed_grad = jnp.dot(grad_flat, dense_full, preferred_element_type=f32).astype(bf16)
    mixed_flat, proj_grad = attention(segment_ids, rotary_rows(segment_ids), proj, mixed_grad)

    qkv_grad = jnp.einsum("nd,jne->jde", attn_flat, proj_grad, preferred_element_type=f32)
    dense_grad = jnp.einsum("nd,ne->de", grad_flat, mixed_flat, preferred_element_type=f32)
    attn_input_grad = jnp.einsum("jne,jde->nd", proj_grad, qkv_full, preferred_element_type=f32)
    mlp_input_grad = jnp.einsum("nf,df->nd", pre_grad, in_full, preferred_element_type=f32)
    normed_grad = (attn_input_grad * gains[0] + mlp_input_grad * gains[1]).reshape(
        seq_count, row_len, model_width
    )
    normed_grad = share_rows(normed_grad, parts)
    vectors = jnp.stack(
        [
            jnp.sum(attn_input_grad * xhat, axis=0),
            jnp.sum(mlp_input_grad * xhat, axis=0),
            jnp.sum(attn_input_grad, axis=0),
            jnp.sum(mlp_input_grad, axis=0),
            jnp.sum(out_grad.astype(f32), axis=(0, 1)),
        ]
    )
    if parts == 2:
        vectors = vectors + lax.ppermute(vectors, "tp", [(0, 1), (1, 0)])
    else:
        vectors = lax.psum(vectors, "tp")
    qkv_bias_grad = jnp.sum(proj_grad.astype(f32), axis=1)
    in_bias_grad = jnp.sum(pre_grad.astype(f32), axis=0)
    small_grads = jnp.concatenate(
        [
            vectors.reshape(5, shards, own_features).transpose(1, 0, 2).reshape(shards, -1),
            qkv_bias_grad.reshape(3, shards, own_bias).transpose(1, 0, 2).reshape(shards, -1),
            in_bias_grad.reshape(shards, own_hidden),
        ],
        axis=1,
    ).astype(bf16)
    attn_grads = jnp.concatenate(
        [qkv_grad[j].astype(bf16).reshape(shards, own_rows, local_width) for j in range(3)]
        + [dense_grad.astype(bf16).reshape(shards, own_rows, local_width)]
        + [pad_rows(small_grads, local_width)],
        axis=1,
    )
    attn_owned = lax.psum_scatter(
        attn_grads.reshape(-1, local_width), "fsdp", scatter_dimension=0, tiled=True
    )

    attn_part = jnp.einsum("ne,de->nd", mixed_flat, dense_full, preferred_element_type=f32)
    mlp_part = jnp.einsum("nf,df->nd", act_low, out_full, preferred_element_type=f32)
    branches = share_rows((attn_part + mlp_part).reshape(seq_count, row_len, model_width), parts)
    local_rows = hidden_in.astype(f32)
    hidden_out = (local_rows + branches + out_shift[0] + out_shift[1]).astype(bf16)

    local_centered = local_rows - jnp.mean(local_rows, axis=-1, keepdims=True)
    local_spread = lax.rsqrt(
        jnp.mean(local_centered * local_centered, axis=-1, keepdims=True) + norm_eps
    )
    local_hat = local_centered * local_spread
    inner = jnp.mean(normed_grad * local_hat, axis=-1, keepdims=True)
    level = jnp.mean(normed_grad, axis=-1, keepdims=True)
    input_grad = out_grad.astype(f32) + (normed_grad - level - local_hat * inner) * local_spread

    owned = attn_owned[: 4 * own_rows].astype(f32).reshape(4, own_rows, local_width)
    small_owned = attn_owned[4 * own_rows :].astype(f32).ravel()
    vector_owned = small_owned[: 5 * own_features].reshape(5, own_features)
    at = 5 * own_features
    bias_owned = small_owned[at : at + 3 * own_bias].reshape(3, own_bias)
    at = at + 3 * own_bias
    hidden_owned = small_owned[at : at + own_hidden]
    return (
        hidden_out,
        input_grad,
        vector_owned[0:2],
        vector_owned[2:4],
        owned[0:3].transpose(1, 0, 2),
        bias_owned,
        owned[3],
        mlp_owned[:own_rows].astype(f32),
        hidden_owned,
        mlp_owned[own_rows:].astype(f32),
        jnp.stack([vector_owned[4], vector_owned[4]]),
    )


def solution(mesh):
    in_specs = (
        P("fsdp", "tp", None),
        P("fsdp", None),
        P(None, "fsdp"),
        P(None, "fsdp"),
        P("fsdp", None, "tp"),
        P(None, ("tp", "fsdp")),
        P("fsdp", "tp"),
        P("fsdp", "tp"),
        P(("tp", "fsdp")),
        P("fsdp", "tp"),
        P(None, "fsdp"),
        P("fsdp", "tp", None),
    )
    out_specs = (
        P("fsdp", "tp", None),
        P("fsdp", "tp", None),
        P(None, "fsdp"),
        P(None, "fsdp"),
        P("fsdp", None, "tp"),
        P(None, ("tp", "fsdp")),
        P("fsdp", "tp"),
        P("fsdp", "tp"),
        P(("tp", "fsdp")),
        P("fsdp", "tp"),
        P(None, "fsdp"),
    )
    return jax.shard_map(
        functools.partial(on_device, mesh.shape["fsdp"], mesh.shape["tp"]),
        mesh=mesh,
        in_specs=in_specs,
        out_specs=out_specs,
        check_vma=False,
    )
```
